32 devices in a mesh: dp: 8 (over z, x), tensor: 2 (over core), group: 2 (over y).
Axes of the slice: x: 2, y: 2, z: 4, core: 2. Of those that a mesh axis runs over, the one named last changes fastest.
Arguments:
- ref_image: bfloat16 [1024, 768], P(('dp', 'tensor')), may hold values from -100 to 100
- ref_text: bfloat16 [1024, 768], P(('dp', 'tensor')), may hold values from -100 to 100
- learner_image: bfloat16 [1024, 1024], P(('dp', 'tensor')), may hold values from -100 to 100
- learner_text: bfloat16 [1024, 1024], P(('dp', 'tensor')), may hold values from -100 to 100
- patches: bfloat16 [1024, 16, 1024], P('dp', 'group', 'tensor'), may hold values from -6 to 6
- cotangent: bfloat16 [1024, 16, 1024], P('dp', 'group', 'tensor'), may hold values from -6 to 6
- w_up: bfloat16 [1024, 4096], P(None, 'tensor'), may hold values from -0.1875 to 0.1875
- w_down: bfloat16 [4096, 1024], P('tensor'), may hold values from -0.09375 to 0.09375
- counts: int32 [8], P('dp'), may hold values from 1 to 64, 384 in all
- sel_index: int32 [512], P('dp'), may hold values from 0 to 127, as said below
- sel_dest: int32 [512, 1], P('dp'), may hold values from 0 to 7; in each aligned block of 64 rows (0 to 63, 64 to 127, ...) at most 16 rows name the same one
Outputs:
- learnability: float32 [1024], P(('dp', 'tensor'))
- routed_out: bfloat16 [1024, 16, 1024], P('dp', 'group', 'tensor')
- grad_up: float32 [1024, 4096], P(('dp', 'group'), 'tensor')
- grad_down_t: float32 [1024, 4096], P(('dp', 'group'), 'tensor')
The draws below stay inside these ranges and needn't reach their ends.
Inputs may be any that keep to these rules, and one draw needn't show every extreme that they name: `sel_index`: within each aligned block of 64 entries the positions are distinct. `sel_dest`: within each aligned block of 64 rows no shard is named more than 16 times.
All inputs are finite; a program needn't handle non-finite values. No bound on the sum of `counts` on one device may be relied on, other than what follows from the above.
Results may differ from the reference program's by a relative error of at most 0.012.
Values may be sent and summed in bfloat16 or wider, within the bound.
A program may use at most 128 MiB of HBM per device.

```python
import math
import jax
import jax.numpy as jnp
import numpy as np
from jax import lax

DR = 768
DL = 1024
FF = 4096
PD = 128
PT = 16
SEL_DEV = 64
CAP = 16
PAIRS = 1024
ROUTED = 1024
N_DP = 8


def shared_parts(key, width, model):
    topic_ids = jax.random.randint(jax.random.fold_in(key, 11), (PAIRS,), 0, 64)
    topic_table = jnp.clip(jax.random.normal(jax.random.fold_in(key, 20 + model), (64, width), jnp.float32), -4.0, 4.0)
    content = jnp.clip(jax.random.normal(jax.random.fold_in(key, 30 + model), (PAIRS, width), jnp.float32), -4.0, 4.0)
    alignment = jax.random.uniform(jax.random.fold_in(key, 40 + model), (PAIRS, 1), jnp.float32)
    return (topic_table[topic_ids], content, alignment)


def blend(shared, private_noise, row_scale):
    topic_rows, content, alignment = shared
    mixed = topic_rows + jnp.sqrt(alignment) * content + jnp.sqrt(1.0 - alignment) * private_noise
    return (row_scale * mixed).astype(jnp.bfloat16)


def embedding(key, width, model, constant):
    shared = shared_parts(key, width, model)
    own_key = jax.random.fold_in(key, constant)
    noise_key = jax.random.fold_in(own_key, 1)
    scale_key = jax.random.fold_in(own_key, 2)
    private_noise = jnp.clip(jax.random.normal(noise_key, (PAIRS, width), jnp.float32), -4.0, 4.0)
    row_scale = jnp.exp(jax.random.uniform(scale_key, (PAIRS, 1), jnp.float32, 0.0, math.log(10.0)))
    return blend(shared, private_noise, row_scale)


def draw_ref_image(key, part):
    return embedding(key, DR, 0, 1)


def draw_ref_text(key, part):
    return embedding(key, DR, 0, 2)


def draw_learner_image(key, part):
    return embedding(key, DL, 1, 3)


def draw_learner_text(key, part):
    return embedding(key, DL, 1, 4)


def draw_sel_index(key, part):
    key = jax.random.fold_in(key, 7)
    keys = jax.random.split(key, N_DP)

    def one_block(block_key):
        order = jax.random.permutation(block_key, PD)[:SEL_DEV]
        return (order + (PD - 1 - order[0])) % PD
    return jax.vmap(one_block)(keys).reshape(-1).astype(jnp.int32)


def shard_levels(stream_key, shape, cuts, smallest, largest):
    loudness = 1.0
    for dim, shards_of in cuts:
        steps = jax.random.uniform(jax.random.fold_in(jax.random.fold_in(stream_key, 6), dim), (shards_of,), jnp.float32, smallest / len(cuts), largest / len(cuts))
        loudness = loudness * jnp.repeat(jnp.exp(steps), shape[dim] // shards_of).reshape((-1,) + (1,) * (len(shape) - 1 - dim))
    return loudness


def length_profile(count, total, bound, slope):
    loads = [(1 << 20) // math.isqrt(grade ** slope) + 1 for grade in range(2, count + 1)]
    spare, given = total - bound - (count - 1), [1] * (count - 1)
    while spare > 0:
        free = [i for i in range(count - 1) if given[i] < bound]
        pool, budget = sum([loads[i] for i in free]), spare
        for i in free:
            addition = min(bound - given[i], max(1, budget * loads[i] // pool), spare)
            given[i] = given[i] + addition
            spare = spare - addition
    return np.array([bound] + given)


def uneven_parts(rng, count, total, limit, slope):
    if count == 2:
        one = jax.random.randint(rng, (), max(1, total - limit), min(limit, total - 1) + 1)
        return jnp.stack([one, total - one])
    lengths = jnp.asarray(length_profile(count, total, limit, slope), jnp.int32)
    pairs = (count - 1) // 2
    giver, taker = lengths[1:1 + 2 * pairs:2], lengths[2:2 + 2 * pairs:2]
    slack = jnp.minimum(giver - 1, limit - taker)
    moved = jax.random.randint(jax.random.fold_in(rng, 1), (pairs,), 0, 1 << 20) % (slack + 1)
    lengths = lengths.at[1:1 + 2 * pairs:2].set(giver - moved).at[2:2 + 2 * pairs:2].set(taker + moved)
    return lengths[jax.random.permutation(jax.random.fold_in(rng, 2), count)]


def assign_block(key, own, number, rows, amount, top, limit, lean):
    sequence = jax.random.permutation(key, amount)
    crowded, common = portions_of(amount, rows * top, limit, lean, True), portions_of(amount, rows * top, limit, lean, False)
    places = jnp.arange(amount)

    def named(tallies, turn):
        used = int((tallies > 0).sum())
        fixed = max(1, used // 4)
        passed = fixed + (places - fixed + turn * (used - fixed)) % max(1, amount - fixed)
        return jnp.zeros((amount,), jnp.int32).at[sequence[jnp.where(places < fixed, places, passed)]].set(jnp.asarray(tallies, jnp.int32))

    tallies = jnp.where(number % 4 == 0, named(crowded, number // 4), named(common, number - number // 4 - 1))
    mixed = jax.random.permutation(jax.random.fold_in(own, 3), amount)
    source_of, sink = mixed[0:amount // 2 * 2:2], mixed[1:amount // 2 * 2:2]
    room = jnp.minimum(tallies[source_of] - 1, limit - tallies[sink]) // 2
    room = jnp.where((source_of == sequence[0]) | (sink == sequence[0]) | (tallies[sink] == 0), 0, jnp.maximum(room, 0))
    passed = jax.random.randint(jax.random.fold_in(own, 4), (amount // 2,), 0, 1 << 20) % (room + 1)
    tallies = tallies.at[source_of].add(-passed).at[sink].add(passed)
    labels = jnp.searchsorted(jnp.cumsum(tallies), jnp.arange(rows * top), side="right").astype(jnp.int32)
    table = labels.reshape(top, rows).T
    table = table[jax.random.permutation(jax.random.fold_in(own, 1), rows)]
    turn = jax.random.randint(jax.random.fold_in(own, 2), (rows, 1), 0, top)
    return jnp.take_along_axis(table, (jnp.arange(top)[None, :] + turn) % top, axis=1)


def portions_of(number_of, total, bound, lean, full):
    weights = [(1 << 20) // math.isqrt(grade ** lean) + 1 for grade in range(1, number_of + 1)]
    largest = bound if full else min(bound, max(-(-total // number_of), total * weights[0] // sum(weights)))
    least = 1 if total - largest >= number_of - 1 else 0
    given, rest = [largest] + [least] * (number_of - 1), total - largest - least * (number_of - 1)
    while rest > 0:
        free = [i for i in range(1, number_of) if given[i] < largest] or [i for i in range(1, number_of) if given[i] < bound]
        whole, budget = sum([weights[i] for i in free]), rest
        for i in free:
            addition = min(bound - given[i], max(1, budget * weights[i] // whole), rest)
            given[i] = given[i] + addition
            rest = rest - addition
    return np.array(given)


def scatter_about(key, shape, spread, bound, cuts=(), kind=jnp.bfloat16):
    entries = jax.random.normal(key, shape, jnp.float32) * spread
    if len(cuts) > 0:
        entries = shard_levels(key, shape, cuts, -0.22, 0.18) * entries
    return jnp.clip(entries, min=-bound, max=bound).astype(kind)


def setup_inputs(seed: int = 0) -> dict:
    splits = jax.random.split(jax.random.key(seed), 12)
    ref_image = draw_ref_image(jax.random.fold_in(splits[11], 71), 0)
    ref_text = draw_ref_text(jax.random.fold_in(splits[11], 71), 0)
    learner_image = draw_learner_image(jax.random.fold_in(splits[11], 71), 0)
    learner_text = draw_learner_text(jax.random.fold_in(splits[11], 71), 0)
    patches = scatter_about(splits[4], (PAIRS, PT, DL), 1.0, 6.0, ((0, 8), (1, 2), (2, 2)))
    cotangent = scatter_about(splits[5], (PAIRS, PT, DL), 1.0, 6.0, ((0, 8), (1, 2), (2, 2)))
    w_up = scatter_about(splits[6], (DL, FF), DL ** -0.5, 0.1875, ((1, 2),))
    w_down = scatter_about(splits[7], (FF, DL), FF ** -0.5, 0.09375, ((0, 2),))
    counts = uneven_parts(splits[8], N_DP, 3 * SEL_DEV * N_DP // 4, SEL_DEV, 2).astype(jnp.int32)
    sel_index = draw_sel_index(jax.random.fold_in(splits[11], 71), 0)
    sel_dest_keys = jax.random.split(jax.random.fold_in(splits[10], 1), (N_DP * SEL_DEV) // SEL_DEV)
    sel_dest_turns = jax.random.permutation(jax.random.fold_in(splits[10], 3), (N_DP * SEL_DEV) // SEL_DEV)
    sel_dest = jax.vmap(lambda own, number: assign_block(jax.random.fold_in(splits[10], 2), own, number, SEL_DEV, N_DP, 1, CAP, 2))(sel_dest_keys, sel_dest_turns).reshape((N_DP * SEL_DEV, 1))
    return {"ref_image": ref_image, "ref_text": ref_text, "learner_image": learner_image, "learner_text": learner_text, "patches": patches, "cotangent": cotangent, "w_up": w_up, "w_down": w_down, "counts": counts, "sel_index": sel_index, "sel_dest": sel_dest}


def unit_rows(block):
    wide = block.astype(jnp.float32)
    return (wide * lax.rsqrt(lax.optimization_barrier(jnp.sum(wide * wide, axis=1, keepdims=True)) + 1e-06)).astype(jnp.bfloat16)

def pair_losses(image, text, temp, bias):
    unit_img = unit_rows(image)
    unit_txt = unit_rows(text)
    scores = temp * jnp.dot(unit_img, unit_txt.T, preferred_element_type=jnp.float32) + bias
    count = scores.shape[0]
    same = jnp.arange(count, dtype=jnp.int32)[:, None] == jnp.arange(count, dtype=jnp.int32)[None, :]
    terms = jnp.where(same, jax.nn.softplus(-scores), jax.nn.softplus(scores))
    return 0.5 * (lax.optimization_barrier(jnp.sum(terms, axis=1)) + lax.optimization_barrier(jnp.sum(terms, axis=0)))

def reference(ref_image, ref_text, learner_image, learner_text, patches, cotangent, w_up, w_down, counts, sel_index, sel_dest):
    learnability = pair_losses(learner_image, learner_text, 10.0, -5.0) - pair_losses(ref_image, ref_text, 10.0, -5.0)
    chosen = sel_index.reshape(N_DP, SEL_DEV)
    target = sel_dest.reshape(N_DP, SEL_DEV)
    live = jnp.arange(SEL_DEV, dtype=jnp.int32)[None, :] < counts[:, None]
    hits = ((target[:, :, None] == jnp.arange(N_DP, dtype=jnp.int32)[None, None, :]) & live[:, :, None]).astype(jnp.int32)
    rank = lax.optimization_barrier(jnp.sum((jnp.cumsum(hits, axis=1) - hits) * hits, axis=2))
    source = jnp.arange(N_DP, dtype=jnp.int32)[:, None]
    pair_ids = (source * PD + chosen).astype(jnp.int32)
    weight = jnp.where(live, jax.nn.sigmoid(learnability[pair_ids]), 0.0).astype(jnp.float32)
    row_ids = jnp.where(live, target * (N_DP * CAP) + source * CAP + rank, ROUTED).astype(jnp.int32)

    def one_source(totals, item):
        ids, pair_weight = item
        block = patches[ids].reshape(SEL_DEV * PT, DL)
        scaled = (pair_weight[:, None, None] * cotangent[ids].astype(jnp.float32)).astype(jnp.bfloat16).reshape(SEL_DEV * PT, DL)
        pre = jnp.dot(block, w_up, preferred_element_type=jnp.float32)
        act_full, gelu_back = jax.vjp(jax.nn.gelu, pre)
        act = act_full.astype(jnp.bfloat16)
        out = (block.astype(jnp.float32) + jnp.dot(act, w_down, preferred_element_type=jnp.float32)).astype(jnp.bfloat16)
        back = jnp.dot(scaled, w_down.T, preferred_element_type=jnp.float32)
        grad_pre = gelu_back(back)[0].astype(jnp.bfloat16)
        grad_up = totals[0] + jnp.dot(block.T, grad_pre, preferred_element_type=jnp.float32)
        grad_down_t = totals[1] + jnp.dot(scaled.T, act, preferred_element_type=jnp.float32)
        return ((grad_up, grad_down_t), out.reshape(SEL_DEV, PT, DL))
    zeros = jnp.zeros((DL, FF), jnp.float32)
    (grad_up, grad_down_t), outs = lax.scan(one_source, (zeros, zeros), (pair_ids, weight))
    routed = jnp.zeros((ROUTED, PT, DL), jnp.bfloat16).at[row_ids.reshape(-1)].set(outs.reshape(-1, PT, DL), mode='drop')
    return (learnability, routed, grad_up, grad_down_t)
```

```python
import jax
import jax.numpy as jnp
from jax import lax
from jax.sharding import PartitionSpec as P


def swap(block, axes, mask):
    names = tuple(axes)
    sizes = [lax.axis_size(name) for name in names]
    total = 1
    for size in sizes:
        total *= size
    route = []
    for start in range(total):
        rest, end, scale = start, 0, 1
        for size, bits in zip(reversed(sizes), reversed(mask)):
            end += ((rest % size) ^ bits) * scale
            rest //= size
            scale *= size
        route.append((start, end))
    return lax.ppermute(block, names if len(names) > 1 else names[0], route)


def unit_rows(block):
    wide = block.astype(jnp.float32)
    return (wide * lax.rsqrt(jnp.sum(wide * wide, axis=1, keepdims=True) + 1e-06)).astype(
        jnp.bfloat16
    )


def loss_parts(image, text, temp, bias):
    rows = image.shape[0]
    far = lax.axis_size("dp") // 2
    near_masks = [(0, 0), (0, 1), (1, 0), (1, 1)]
    images = [image] + [swap(image, ("dp", "tensor"), mask) for mask in near_masks[1:]]
    texts = [text] + [swap(text, ("dp",), (2 * mask,)) for mask in range(1, far)]
    img = jnp.concatenate(images, axis=0)
    txt = jnp.concatenate(texts, axis=0)
    scores = temp * jnp.einsum("rd,kd->rk", img, txt, preferred_element_type=jnp.float32) + bias
    at_row = jnp.arange(img.shape[0], dtype=jnp.int32)[:, None]
    at_col = jnp.arange(txt.shape[0], dtype=jnp.int32)[None, :]
    same = (at_row == at_col) & (at_row < rows)
    terms = jax.nn.softplus(jnp.where(same, -scores, scores))
    by_image = jnp.sum(terms, axis=1).reshape(2, 2, rows)
    by_text = jnp.sum(terms, axis=0).reshape(far, rows)
    of_shard = by_image[0] + swap(by_image[1], ("dp",), (1,))
    of_text = by_text[0]
    for mask in range(1, far):
        of_text = of_text + swap(by_text[mask], ("dp",), (2 * mask,))
    return 0.5 * jnp.stack([of_shard[0] + of_text, of_shard[1]])


def scatter_sum(block, order, axis_bits):
    bits = len(axis_bits)
    width = block.shape[1]
    cut = block.reshape((2,) * bits + (-1, width))
    left = list(range(bits))
    for step, bit in enumerate(order):
        name, mask = axis_bits[bit]
        mine = (lax.axis_index(name) // mask) % 2
        at = left.index(bit)
        left.remove(bit)
        keep = lax.dynamic_index_in_dim(cut, mine, at, keepdims=False)
        send = lax.dynamic_index_in_dim(cut, 1 - mine, at, keepdims=False)
        came = swap(send, (name,), (mask,))
        cut = keep.astype(jnp.float32) + came.astype(jnp.float32)
        if step < bits - 1:
            cut = cut.astype(jnp.bfloat16)
    return cut


def part_orders(bits):
    group, near, next_near = bits - 1, bits - 2, bits - 3
    rest = [bit for bit in range(bits - 4, -1, -1)]
    return [
        [near, group, next_near] + rest,
        [group, near, next_near] + rest,
        [next_near, near, group] + rest,
    ]


def local(
    ref_image,
    ref_text,
    learner_image,
    learner_text,
    patches,
    cotangent,
    w_up,
    w_down,
    counts,
    sel_index,
    sel_dest,
):
    group_at = lax.axis_index("group")
    tensor_at = lax.axis_index("tensor")
    dp_at = lax.axis_index("dp")
    n_dp = lax.axis_size("dp")
    extra = learner_image.shape[1] - ref_image.shape[1]
    is_ref = group_at == 0

    def own_model(ref_block, learner_block):
        ref_block = jnp.pad(ref_block, ((0, 0), (0, extra)))
        return unit_rows(jnp.where(is_ref, ref_block, learner_block))

    share = loss_parts(
        own_model(ref_image, learner_image), own_model(ref_text, learner_text), 10.0, -5.0
    )

    slots = sel_index.shape[0]
    cap = max(2, 2 * slots // n_dp)
    patch_rows, half_width = (patches.shape[1], patches.shape[2])
    count = slots * patch_rows
    half_x = patches[sel_index].reshape(count, half_width)
    half_cot = cotangent[sel_index].reshape(count, half_width)

    def widen(half):
        other = swap(half, ("tensor",), (1,))
        return jnp.concatenate(
            [jnp.where(tensor_at == 0, half, other), jnp.where(tensor_at == 0, other, half)], axis=1
        )

    x = widen(half_x)
    cot = widen(half_cot)
    pre = jnp.dot(x, w_up, preferred_element_type=jnp.float32)
    act_full, gelu_back = jax.vjp(jax.nn.gelu, pre)
    act = lax.optimization_barrier(act_full.astype(jnp.bfloat16))
    partial_out = jnp.dot(act, w_down, preferred_element_type=jnp.float32)
    back = jnp.einsum("md,fd->mf", cot, w_down, preferred_element_type=jnp.float32)
    grad_pre = lax.optimization_barrier(gelu_back(back)[0])

    halves = partial_out.reshape(count, 2, half_width)
    keep = lax.dynamic_index_in_dim(halves, tensor_at, 1, keepdims=False)
    send = lax.dynamic_index_in_dim(halves, 1 - tensor_at, 1, keepdims=False)
    came = swap(send.astype(jnp.bfloat16), ("tensor",), (1,))
    out = (half_x.astype(jnp.float32) + (keep + came.astype(jnp.float32))).astype(jnp.bfloat16)

    live = jnp.arange(slots, dtype=jnp.int32) < counts[0]
    target = sel_dest[:, 0]
    earlier = jnp.arange(slots)[:, None] > jnp.arange(slots)[None, :]
    rank = jnp.sum(
        (earlier & (target[:, None] == target[None, :]) & live[None, :]).astype(jnp.int32), axis=1
    )
    bucket = (target ^ dp_at) * cap + rank
    placer = (
        (jnp.arange(n_dp * cap, dtype=jnp.int32)[:, None] == bucket[None, :]) & live[None, :]
    ).astype(jnp.bfloat16)
    boxed = jnp.dot(
        placer, out.reshape(slots, patch_rows * half_width), preferred_element_type=jnp.float32
    ).astype(jnp.bfloat16)
    boxed = boxed.reshape(n_dp, cap, patch_rows, half_width)
    landed = jnp.stack(
        [boxed[0]] + [swap(boxed[mask], ("dp",), (mask,)) for mask in range(1, n_dp)]
    )
    routed = landed[jnp.arange(n_dp, dtype=jnp.int32) ^ dp_at].reshape(
        n_dp * cap, patch_rows, half_width
    )

    share = jnp.where(tensor_at == 0, share, share[::-1])
    mine = share + swap(share, ("tensor",), (1,))
    partner = swap(share, ("group",), (1,)) + swap(share, ("tensor", "group"), (1, 1))
    shard_scores = jnp.where(is_ref, partner - mine, mine - partner)
    learnability = lax.dynamic_index_in_dim(shard_scores, tensor_at, 0, keepdims=False)
    picked = sel_index[:, None] == jnp.arange(patches.shape[0], dtype=jnp.int32)[None, :]
    score_sel = jnp.sum(jnp.where(picked, shard_scores.reshape(1, -1), 0.0), axis=1)
    weight = jnp.where(live, jax.nn.sigmoid(score_sel), 0.0)
    row_weight = jnp.repeat(weight, patch_rows)[:, None]

    axis_bits = [("dp", 1 << bit) for bit in range(n_dp.bit_length() - 2, -1, -1)] + [("group", 1)]
    hidden = w_up.shape[1]
    edges = [0, hidden * 3 // 8, hidden * 3 // 4, hidden]
    orders = part_orders(len(axis_bits))
    sums = []
    for rows, cols in ((x, grad_pre), (cot, act)):
        scaled = (row_weight * cols.astype(jnp.float32)).astype(jnp.bfloat16)
        parts = []
        for order, low, high in zip(orders, edges[:-1], edges[1:]):
            product = jnp.einsum(
                "md,mf->df", rows, scaled[:, low:high], preferred_element_type=jnp.float32
            ).astype(jnp.bfloat16)
            parts.append(scatter_sum(product, order, axis_bits))
        sums.append(jnp.concatenate(parts, axis=1))
    return (learnability, routed, sums[0], sums[1])


def solution(mesh):
    placed = (
        P(("dp", "tensor"), None),
        P(("dp", "tensor"), None),
        P(("dp", "tensor"), None),
        P(("dp", "tensor"), None),
        P("dp", "group", "tensor"),
        P("dp", "group", "tensor"),
        P(None, "tensor"),
        P("tensor", None),
        P("dp"),
        P("dp"),
        P("dp", None),
    )
    return jax.shard_map(
        local,
        mesh=mesh,
        in_specs=placed,
        out_specs=(
            P(("dp", "tensor")),
            P("dp", "group", "tensor"),
            P(("dp", "group"), "tensor"),
            P(("dp", "group"), "tensor"),
        ),
        check_vma=False,
    )
```

```python
import itertools
import jax
import jax.numpy as jnp
from jax import lax
from jax.experimental import pallas as pl
from jax.experimental.pallas import tpu as pltpu
from jax.sharding import PartitionSpec as P


def swap(block, axes, mask):
    names = tuple(axes)
    sizes = [lax.axis_size(name) for name in names]
    total = 1
    for size in sizes:
        total *= size
    route = []
    for start in range(total):
        rest, end, scale = start, 0, 1
        for size, bits in zip(reversed(sizes), reversed(mask)):
            end += ((rest % size) ^ bits) * scale
            rest //= size
            scale *= size
        route.append((start, end))
    return lax.ppermute(block, names if len(names) > 1 else names[0], route)


def unit_rows(block):
    wide = block.astype(jnp.float32)
    return (wide * lax.rsqrt(jnp.sum(wide * wide, axis=1, keepdims=True) + 1e-06)).astype(
        jnp.bfloat16
    )


def loss_parts(image, text, temp, bias):
    rows = image.shape[0]
    far = lax.axis_size("dp") // 2
    near_masks = [(0, 0), (0, 1), (1, 0), (1, 1)]
    images = [image] + [swap(image, ("dp", "tensor"), mask) for mask in near_masks[1:]]
    texts = [text] + [swap(text, ("dp",), (2 * mask,)) for mask in range(1, far)]
    img = jnp.concatenate(images, axis=0)
    txt = jnp.concatenate(texts, axis=0)
    scores = temp * jnp.einsum("rd,kd->rk", img, txt, preferred_element_type=jnp.float32) + bias
    at_row = jnp.arange(img.shape[0], dtype=jnp.int32)[:, None]
    at_col = jnp.arange(txt.shape[0], dtype=jnp.int32)[None, :]
    same = (at_row == at_col) & (at_row < rows)
    terms = jax.nn.softplus(jnp.where(same, -scores, scores))
    by_image = jnp.sum(terms, axis=1).reshape(2, 2, rows)
    by_text = jnp.sum(terms, axis=0).reshape(far, rows)
    of_shard = by_image[0] + swap(by_image[1], ("dp",), (1,))
    of_text = by_text[0]
    for mask in range(1, far):
        of_text = of_text + swap(by_text[mask], ("dp",), (2 * mask,))
    return 0.5 * jnp.stack([of_shard[0] + of_text, of_shard[1]])


def flip(index, mask):
    out, bit = index, 1
    while bit <= mask:
        if mask & bit:
            out = out + bit * (1 - 2 * ((index // bit) % 2))
        bit *= 2
    return out


def grad_kernel(
    axis_bits, orders, widths, subs, n_dp,
    xt_ref, ct_ref, dh_ref, act_ref, boxed_ref,
    up_ref, down_ref, landed_ref,
    *scratch,
):
    bits, kinds = len(axis_bits), len(orders)
    prods = scratch[:kinds]
    recvs = [scratch[kinds + kind * bits : kinds + (kind + 1) * bits] for kind in range(kinds)]
    send_sem, recv_sem, box_send, box_recv = scratch[kinds + kinds * bits :]
    dp_at = lax.axis_index("dp")
    group_at = lax.axis_index("group")
    at = {"dp": dp_at, "group": group_at}

    barrier = pltpu.get_barrier_semaphore()
    partners = [{"dp": flip(dp_at, mask)} for mask in range(1, n_dp)]
    partners.append({"group": 1 - group_at})
    for partner in partners:
        pl.semaphore_signal(
            barrier, inc=1, device_id=partner, device_id_type=pl.DeviceIdType.MESH
        )
    pl.semaphore_wait(barrier, len(partners))

    def pick(ref, lead, left, bit, value):
        place = [slice(None)] * len(left)
        place[left.index(bit)] = value
        return ref.at[tuple(lead + place)]

    def source(kind, step):
        return prods[kind] if step == 0 else recvs[kind][step - 1]

    def exchange(kind, turn, step):
        bit = orders[kind][step]
        left = [other for other in range(bits) if other not in orders[kind][:step]]
        name, mask = axis_bits[bit]
        mine = (at[name] // mask) % 2
        ref = source(kind, step)
        copy = pltpu.make_async_remote_copy(
            src_ref=pick(ref, [turn], left, bit, 1 - mine),
            dst_ref=recvs[kind][step].at[turn],
            send_sem=send_sem.at[kind, turn, step],
            recv_sem=recv_sem.at[kind, turn, step],
            device_id={name: flip(at[name], mask)},
            device_id_type=pl.DeviceIdType.MESH,
        )
        return copy, pick(ref, [turn], left, bit, mine)

    turns = 2 * subs
    starts = [subs * sum(widths[:kind]) for kind in range(kinds)]
    flight = {}
    for turn in range(turns):
        rows_ref, cols_ref = ((xt_ref, dh_ref), (ct_ref, act_ref))[turn // subs]
        for kind in range(kinds):
            width = widths[kind]
            low = starts[kind] + (turn % subs) * width
            tile = rows_ref.shape[0] // 4

            def multiply(tile_at, carry, kind=kind, turn=turn, low=low, width=width,
                         rows_ref=rows_ref, cols_ref=cols_ref, tile=tile):
                product = jnp.dot(
                    rows_ref[pl.ds(pl.multiple_of(tile_at * tile, tile), tile), :],
                    cols_ref[:, low : low + width],
                    preferred_element_type=jnp.float32,
                )
                dest = prods[kind].at[turn, tile_at // 2, tile_at % 2]
                dest[...] = product.astype(jnp.bfloat16).reshape(dest.shape)
                return carry

            lax.fori_loop(0, 4, multiply, 0)
            copy, keep = exchange(kind, turn, 0)
            copy.start()
            flight[kind, turn] = (copy, keep)

    boxes = []
    for mask in range(1, n_dp):
        box = pltpu.make_async_remote_copy(
            src_ref=boxed_ref.at[mask],
            dst_ref=landed_ref.at[mask],
            send_sem=box_send.at[mask],
            recv_sem=box_recv.at[mask],
            device_id={"dp": flip(dp_at, mask)},
            device_id_type=pl.DeviceIdType.MESH,
        )
        box.start()
        boxes.append(box)
    landed_ref[0] = boxed_ref[0]

    sent = []
    for step in range(bits):
        for turn in range(turns):
            for kind in range(kinds):
                copy, keep = flight[kind, turn]
                copy.wait_recv()
                sent.append(copy)
                came = recvs[kind][step].at[turn]
                if step < bits - 1:
                    for lead in itertools.product(*[range(size) for size in came.shape[:-2]]):
                        came[lead] = (
                            came[lead].astype(jnp.float32) + keep[lead].astype(jnp.float32)
                        ).astype(jnp.bfloat16)
                    copy, keep = exchange(kind, turn, step + 1)
                    copy.start()
                    flight[kind, turn] = (copy, keep)
                else:
                    out_ref = (up_ref, down_ref)[turn // subs]
                    low = starts[kind] + (turn % subs) * widths[kind]
                    out_ref[:, low : low + widths[kind]] = came[...].astype(jnp.float32) + keep[
                        ...
                    ].astype(jnp.float32)
    for copy in sent:
        copy.wait_send()
    for box in boxes:
        box.wait()


def gradients(xt, ct, dh, act, boxed, axis_bits):
    bits = len(axis_bits)
    orders = part_orders(bits)
    depth, hidden = dh.shape
    subs = 2
    widths = [hidden * 3 // 8 // subs, hidden * 3 // 8 // subs, hidden // 4 // subs]
    turns = 2 * subs
    rows = xt.shape[0] >> bits
    n_dp = boxed.shape[0]
    prods = [
        pltpu.VMEM((turns,) + (2,) * bits + (rows, width), jnp.bfloat16) for width in widths
    ]
    recvs = [
        pltpu.VMEM((turns,) + (2,) * (bits - 1 - step) + (rows, width), jnp.bfloat16)
        for width in widths
        for step in range(bits)
    ]
    vmem = pl.BlockSpec(memory_space=pltpu.VMEM)
    kernel = lambda *refs: grad_kernel(axis_bits, orders, widths, subs, n_dp, *refs)
    return pl.pallas_call(
        kernel,
        out_shape=(
            jax.ShapeDtypeStruct((rows, hidden), jnp.float32),
            jax.ShapeDtypeStruct((rows, hidden), jnp.float32),
            jax.ShapeDtypeStruct(boxed.shape, boxed.dtype),
        ),
        in_specs=[vmem] * 5,
        out_specs=(vmem, vmem, vmem),
        scratch_shapes=prods
        + recvs
        + [
            pltpu.SemaphoreType.DMA((len(orders), turns, bits)),
            pltpu.SemaphoreType.DMA((len(orders), turns, bits)),
            pltpu.SemaphoreType.DMA((n_dp,)),
            pltpu.SemaphoreType.DMA((n_dp,)),
        ],
        compiler_params=pltpu.CompilerParams(
            collective_id=0, has_side_effects=True, vmem_limit_bytes=44 * 1024 * 1024
        ),
        cost_estimate=pl.CostEstimate(
            flops=4 * xt.shape[0] * depth * hidden, bytes_accessed=1 << 24, transcendentals=0
        ),
        name="grad_sums",
    )(xt, ct, dh, act, boxed)


def part_orders(bits):
    group, near, next_near = bits - 1, bits - 2, bits - 3
    rest = [bit for bit in range(bits - 4, -1, -1)]
    return [
        [near, group, next_near] + rest,
        [group, near, next_near] + rest,
        [next_near, near, group] + rest,
    ]


def local(
    ref_image,
    ref_text,
    learner_image,
    learner_text,
    patches,
    cotangent,
    w_up,
    w_down,
    counts,
    sel_index,
    sel_dest,
):
    group_at = lax.axis_index("group")
    tensor_at = lax.axis_index("tensor")
    dp_at = lax.axis_index("dp")
    n_dp = lax.axis_size("dp")
    extra = learner_image.shape[1] - ref_image.shape[1]
    is_ref = group_at == 0

    def own_model(ref_block, learner_block):
        ref_block = jnp.pad(ref_block, ((0, 0), (0, extra)))
        return unit_rows(jnp.where(is_ref, ref_block, learner_block))

    share = loss_parts(
        own_model(ref_image, learner_image), own_model(ref_text, learner_text), 10.0, -5.0
    )

    slots = sel_index.shape[0]
    cap = max(2, 2 * slots // n_dp)
    patch_rows, half_width = (patches.shape[1], patches.shape[2])
    count = slots * patch_rows
    half_x = patches[sel_index].reshape(count, half_width)
    half_cot = cotangent[sel_index].reshape(count, half_width)

    def widen(half):
        other = swap(half, ("tensor",), (1,))
        return jnp.concatenate(
            [jnp.where(tensor_at == 0, half, other), jnp.where(tensor_at == 0, other, half)], axis=1
        )

    x = widen(half_x)
    cot = widen(half_cot)
    pre = jnp.dot(x, w_up, preferred_element_type=jnp.float32)
    act_full, gelu_back = jax.vjp(jax.nn.gelu, pre)
    act = lax.optimization_barrier(act_full.astype(jnp.bfloat16))
    partial_out = jnp.dot(act, w_down, preferred_element_type=jnp.float32)
    back = jnp.einsum("md,fd->mf", cot, w_down, preferred_element_type=jnp.float32)
    grad_pre = lax.optimization_barrier(gelu_back(back)[0])

    halves = partial_out.reshape(count, 2, half_width)
    keep = lax.dynamic_index_in_dim(halves, tensor_at, 1, keepdims=False)
    send = lax.dynamic_index_in_dim(halves, 1 - tensor_at, 1, keepdims=False)
    came = swap(send.astype(jnp.bfloat16), ("tensor",), (1,))
    out = (half_x.astype(jnp.float32) + (keep + came.astype(jnp.float32))).astype(jnp.bfloat16)

    live = jnp.arange(slots, dtype=jnp.int32) < counts[0]
    target = sel_dest[:, 0]
    earlier = jnp.arange(slots)[:, None] > jnp.arange(slots)[None, :]
    rank = jnp.sum(
        (earlier & (target[:, None] == target[None, :]) & live[None, :]).astype(jnp.int32), axis=1
    )
    bucket = (target ^ dp_at) * cap + rank
    placer = (
        (jnp.arange(n_dp * cap, dtype=jnp.int32)[:, None] == bucket[None, :]) & live[None, :]
    ).astype(jnp.bfloat16)
    boxed = jnp.dot(
        placer, out.reshape(slots, patch_rows * half_width), preferred_element_type=jnp.float32
    ).astype(jnp.bfloat16)
    boxed = boxed.reshape(n_dp, cap, patch_rows, half_width)
    share = jnp.where(tensor_at == 0, share, share[::-1])
    mine = share + swap(share, ("tensor",), (1,))
    partner = swap(share, ("group",), (1,)) + swap(share, ("tensor", "group"), (1, 1))
    shard_scores = jnp.where(is_ref, partner - mine, mine - partner)
    learnability = lax.dynamic_index_in_dim(shard_scores, tensor_at, 0, keepdims=False)
    picked = sel_index[:, None] == jnp.arange(patches.shape[0], dtype=jnp.int32)[None, :]
    score_sel = jnp.sum(jnp.where(picked, shard_scores.reshape(1, -1), 0.0), axis=1)
    weight = jnp.where(live, jax.nn.sigmoid(score_sel), 0.0)
    row_weight = jnp.repeat(weight, patch_rows)[:, None]

    axis_bits = [("dp", 1 << bit) for bit in range(n_dp.bit_length() - 2, -1, -1)] + [("group", 1)]
    dh = (row_weight * grad_pre).astype(jnp.bfloat16)
    weighted_act = (row_weight * act.astype(jnp.float32)).astype(jnp.bfloat16)
    grad_up, grad_down_t, landed = gradients(
        x.T, cot.T, dh, weighted_act, boxed, axis_bits
    )
    routed = landed[jnp.arange(n_dp, dtype=jnp.int32) ^ dp_at].reshape(
        n_dp * cap, patch_rows, half_width
    )
    return (learnability, routed, grad_up, grad_down_t)


def solution(mesh):
    placed = (
        P(("dp", "tensor"), None),
        P(("dp", "tensor"), None),
        P(("dp", "tensor"), None),
        P(("dp", "tensor"), None),
        P("dp", "group", "tensor"),
        P("dp", "group", "tensor"),
        P(None, "tensor"),
        P("tensor", None),
        P("dp"),
        P("dp"),
        P("dp", None),
    )
    return jax.shard_map(
        local,
        mesh=mesh,
        in_specs=placed,
        out_specs=(
            P(("dp", "tensor")),
            P("dp", "group", "tensor"),
            P(("dp", "group"), "tensor"),
            P(("dp", "group"), "tensor"),
        ),
        check_vma=False,
    )
```

```python
import itertools
import jax
import jax.numpy as jnp
from jax import lax
from jax.experimental import pallas as pl
from jax.experimental.pallas import tpu as pltpu
from jax.sharding import PartitionSpec as P


def swap(block, axes, mask):
    names = tuple(axes)
    sizes = [lax.axis_size(name) for name in names]
    total = 1
    for size in sizes:
        total *= size
    route = []
    for start in range(total):
        rest, end, scale = start, 0, 1
        for size, bits in zip(reversed(sizes), reversed(mask)):
            end += ((rest % size) ^ bits) * scale
            rest //= size
            scale *= size
        route.append((start, end))
    return lax.ppermute(block, names if len(names) > 1 else names[0], route)


def flip(index, mask):
    out, bit = index, 1
    while bit <= mask:
        if mask & bit:
            out = out + bit * (1 - 2 * ((index // bit) % 2))
        bit *= 2
    return out


def loss_kernel(
    n_dp, temp, bias,
    ref_img, ref_txt, own_img, own_txt, half_x, half_cot,
    score_ref, other_x, other_cot,
    imgs, txts, row_out, row_in, text_out, text_in, share, share_in, send_sem, recv_sem,
):
    rows, width = own_img.shape
    far = n_dp // 2
    dp_at, tensor_at = lax.axis_index("dp"), lax.axis_index("tensor")
    group_at = lax.axis_index("group")
    over_tensor = {"tensor": 1 - tensor_at}
    near = [
        over_tensor,
        {"dp": flip(dp_at, 1)},
        {"dp": flip(dp_at, 1), "tensor": 1 - tensor_at},
    ]
    across = [{"dp": flip(dp_at, 2 * mask)} for mask in range(1, far)]
    models = [{"group": 1 - group_at}, {"group": 1 - group_at, "tensor": 1 - tensor_at}]
    partners = near + across + models
    barrier = pltpu.get_barrier_semaphore()
    for partner in partners:
        pl.semaphore_signal(
            barrier, inc=1, device_id=partner, device_id_type=pl.DeviceIdType.MESH
        )

    def put(value, dest):
        wide = value[...].astype(jnp.float32)
        total = jnp.sum(wide * wide, axis=1, keepdims=True)
        dest[:, : value.shape[1]] = (wide * lax.rsqrt(total + 1e-06)).astype(jnp.bfloat16)

    @pl.when(group_at == 0)
    def _():
        for raw, dest in ((ref_img, imgs.at[0]), (ref_txt, txts.at[0])):
            dest[...] = jnp.zeros((rows, width), jnp.bfloat16)
            put(raw, dest)

    @pl.when(group_at == 1)
    def _():
        put(own_img, imgs.at[0])
        put(own_txt, txts.at[0])

    pl.semaphore_wait(barrier, len(partners))
    used = [0]

    def send(src, dest, partner):
        at = used[0]
        used[0] += 1
        copy = pltpu.make_async_remote_copy(
            src_ref=src,
            dst_ref=dest,
            send_sem=send_sem.at[at],
            recv_sem=recv_sem.at[at],
            device_id=partner,
            device_id_type=pl.DeviceIdType.MESH,
        )
        copy.start()
        return copy

    copies = [send(txts.at[0], txts.at[m], to) for m, to in enumerate(across, 1)]
    copies += [send(imgs.at[0], imgs.at[m], to) for m, to in enumerate(near, 1)]
    wide_copies = [send(half_x, other_x, over_tensor), send(half_cot, other_cot, over_tensor)]
    for copy in copies:
        copy.wait()

    def sums(long, short, has_own):
        scores = temp * lax.dot_general(
            long, short, (((1,), (1,)), ((), ())), preferred_element_type=jnp.float32
        ) + bias
        if has_own:
            at_row = lax.broadcasted_iota(jnp.int32, scores.shape, 0)
            at_col = lax.broadcasted_iota(jnp.int32, scores.shape, 1)
            scores = jnp.where(at_row == at_col, -scores, scores)
        terms = jnp.maximum(scores, 0.0) + jnp.log1p(jnp.exp(-jnp.abs(scores)))
        total = jnp.sum(terms, axis=0, keepdims=True)
        total = jnp.concatenate([total, jnp.zeros((1, 128 - rows), jnp.float32)], axis=1)
        return jnp.broadcast_to(total, (8, 128))

    all_txt = txts[...].reshape(far * rows, width)
    all_img = imgs[...].reshape(4 * rows, width)
    by_image = [sums(all_txt, imgs[m], m == 0) for m in range(4)]
    row_out[0] = by_image[2]
    row_out[1] = by_image[3]
    copies = [send(row_out, row_in, near[1])]
    for m in range(1, far):
        text_out[m] = sums(all_img, txts[m], False)
        copies.append(send(text_out.at[m], text_in.at[m], across[m - 1]))
    own_text = sums(all_img, txts[0], True)
    for copy in copies:
        copy.wait()
    for m in range(1, far):
        own_text = own_text + text_in[m]
    share[0] = 0.5 * (by_image[0] + row_in[0] + own_text)
    share[1] = 0.5 * (by_image[1] + row_in[1])
    copies = [
        send(share, share_in.at[m], to) for m, to in enumerate([over_tensor] + models)
    ]
    for copy in copies:
        copy.wait()
    for half in range(2):
        mine = share[half] + share_in[0, 1 - half]
        partner = share_in[1, half] + share_in[2, 1 - half]
        score_ref[half] = jnp.where(group_at == 0, partner - mine, mine - partner)
    for copy in wide_copies:
        copy.wait()


def shard_learnability(ref_img, ref_txt, own_img, own_txt, half_x, half_cot, n_dp):
    rows, width = own_img.shape
    far = n_dp // 2
    copies = 3 + (far - 1) + 2 + 1 + (far - 1) + 3
    vmem = pl.BlockSpec(memory_space=pltpu.VMEM)
    kernel = lambda *refs: loss_kernel(n_dp, 10.0, -5.0, *refs)
    tile = (8, 128)
    return pl.pallas_call(
        kernel,
        out_shape=(
            jax.ShapeDtypeStruct((2,) + tile, jnp.float32),
            jax.ShapeDtypeStruct(half_x.shape, half_x.dtype),
            jax.ShapeDtypeStruct(half_cot.shape, half_cot.dtype),
        ),
        in_specs=[vmem] * 6,
        out_specs=(vmem, vmem, vmem),
        scratch_shapes=[
            pltpu.VMEM((4, rows, width), jnp.bfloat16),
            pltpu.VMEM((far, rows, width), jnp.bfloat16),
            pltpu.VMEM((2,) + tile, jnp.float32),
            pltpu.VMEM((2,) + tile, jnp.float32),
            pltpu.VMEM((far,) + tile, jnp.float32),
            pltpu.VMEM((far,) + tile, jnp.float32),
            pltpu.VMEM((2,) + tile, jnp.float32),
            pltpu.VMEM((3, 2) + tile, jnp.float32),
            pltpu.SemaphoreType.DMA((copies,)),
            pltpu.SemaphoreType.DMA((copies,)),
        ],
        compiler_params=pltpu.CompilerParams(
            collective_id=1, has_side_effects=True, vmem_limit_bytes=24 * 1024 * 1024
        ),
        cost_estimate=pl.CostEstimate(
            flops=16 * rows * rows * far * width, bytes_accessed=1 << 22, transcendentals=1 << 18
        ),
        name="pair_losses",
    )(ref_img, ref_txt, own_img, own_txt, half_x, half_cot)


def grad_kernel(
    axis_bits, orders, widths, subs, n_dp,
    xt_ref, ct_ref, dh_ref, act_ref, boxed_ref,
    up_ref, down_ref, landed_ref,
    *scratch,
):
    bits, kinds = len(axis_bits), len(orders)
    prods = scratch[:kinds]
    recvs = [scratch[kinds + kind * bits : kinds + (kind + 1) * bits] for kind in range(kinds)]
    send_sem, recv_sem, box_send, box_recv = scratch[kinds + kinds * bits :]
    dp_at = lax.axis_index("dp")
    group_at = lax.axis_index("group")
    at = {"dp": dp_at, "group": group_at}

    barrier = pltpu.get_barrier_semaphore()
    partners = [{"dp": flip(dp_at, mask)} for mask in range(1, n_dp)]
    partners.append({"group": 1 - group_at})
    for partner in partners:
        pl.semaphore_signal(
            barrier, inc=1, device_id=partner, device_id_type=pl.DeviceIdType.MESH
        )
    pl.semaphore_wait(barrier, len(partners))

    def pick(ref, lead, left, bit, value):
        place = [slice(None)] * len(left)
        place[left.index(bit)] = value
        return ref.at[tuple(lead + place)]

    def source(kind, step):
        return prods[kind] if step == 0 else recvs[kind][step - 1]

    def exchange(kind, turn, step):
        bit = orders[kind][step]
        left = [other for other in range(bits) if other not in orders[kind][:step]]
        name, mask = axis_bits[bit]
        mine = (at[name] // mask) % 2
        ref = source(kind, step)
        copy = pltpu.make_async_remote_copy(
            src_ref=pick(ref, [turn], left, bit, 1 - mine),
            dst_ref=recvs[kind][step].at[turn],
            send_sem=send_sem.at[kind, turn, step],
            recv_sem=recv_sem.at[kind, turn, step],
            device_id={name: flip(at[name], mask)},
            device_id_type=pl.DeviceIdType.MESH,
        )
        return copy, pick(ref, [turn], left, bit, mine)

    turns = 2 * subs
    starts = [subs * sum(widths[:kind]) for kind in range(kinds)]
    flight = {}
    for turn in range(turns):
        rows_ref, cols_ref = ((xt_ref, dh_ref), (ct_ref, act_ref))[turn // subs]
        for kind in range(kinds):
            width = widths[kind]
            low = starts[kind] + (turn % subs) * width
            tile = rows_ref.shape[0] // 4

            def multiply(tile_at, carry, kind=kind, turn=turn, low=low, width=width,
                         rows_ref=rows_ref, cols_ref=cols_ref, tile=tile):
                product = jnp.dot(
                    rows_ref[pl.ds(pl.multiple_of(tile_at * tile, tile), tile), :],
                    cols_ref[:, low : low + width],
                    preferred_element_type=jnp.float32,
                )
                dest = prods[kind].at[turn, tile_at // 2, tile_at % 2]
                dest[...] = product.astype(jnp.bfloat16).reshape(dest.shape)
                return carry

            lax.fori_loop(0, 4, multiply, 0)
            copy, keep = exchange(kind, turn, 0)
            copy.start()
            flight[kind, turn] = (copy, keep)

    boxes = []
    for mask in range(1, n_dp):
        box = pltpu.make_async_remote_copy(
            src_ref=boxed_ref.at[mask],
            dst_ref=landed_ref.at[dp_at],
            send_sem=box_send.at[mask],
            recv_sem=box_recv.at[mask],
            device_id={"dp": flip(dp_at, mask)},
            device_id_type=pl.DeviceIdType.MESH,
        )
        box.start()
        boxes.append(box)
    landed_ref[dp_at] = boxed_ref[0]

    sent = []
    for step in range(bits):
        for turn in range(turns):
            for kind in range(kinds):
                copy, keep = flight[kind, turn]
                copy.wait_recv()
                sent.append(copy)
                came = recvs[kind][step].at[turn]
                if step < bits - 1:
                    for lead in itertools.product(*[range(size) for size in came.shape[:-2]]):
                        came[lead] = (
                            came[lead].astype(jnp.float32) + keep[lead].astype(jnp.float32)
                        ).astype(jnp.bfloat16)
                    copy, keep = exchange(kind, turn, step + 1)
                    copy.start()
                    flight[kind, turn] = (copy, keep)
                else:
                    out_ref = (up_ref, down_ref)[turn // subs]
                    low = starts[kind] + (turn % subs) * widths[kind]
                    out_ref[:, low : low + widths[kind]] = came[...].astype(jnp.float32) + keep[
                        ...
                    ].astype(jnp.float32)
    for copy in sent:
        copy.wait_send()
    for box in boxes:
        box.wait()


def gradients(xt, ct, dh, act, boxed, axis_bits):
    bits = len(axis_bits)
    orders = part_orders(bits)
    depth, hidden = dh.shape
    subs = 2
    widths = [hidden * 3 // 8 // subs, hidden * 3 // 8 // subs, hidden // 4 // subs]
    turns = 2 * subs
    rows = xt.shape[0] >> bits
    n_dp = boxed.shape[0]
    prods = [
        pltpu.VMEM((turns,) + (2,) * bits + (rows, width), jnp.bfloat16) for width in widths
    ]
    recvs = [
        pltpu.VMEM((turns,) + (2,) * (bits - 1 - step) + (rows, width), jnp.bfloat16)
        for width in widths
        for step in range(bits)
    ]
    vmem = pl.BlockSpec(memory_space=pltpu.VMEM)
    kernel = lambda *refs: grad_kernel(axis_bits, orders, widths, subs, n_dp, *refs)
    return pl.pallas_call(
        kernel,
        out_shape=(
            jax.ShapeDtypeStruct((rows, hidden), jnp.float32),
            jax.ShapeDtypeStruct((rows, hidden), jnp.float32),
            jax.ShapeDtypeStruct(boxed.shape, boxed.dtype),
        ),
        in_specs=[vmem] * 5,
        out_specs=(vmem, vmem, vmem),
        scratch_shapes=prods
        + recvs
        + [
            pltpu.SemaphoreType.DMA((len(orders), turns, bits)),
            pltpu.SemaphoreType.DMA((len(orders), turns, bits)),
            pltpu.SemaphoreType.DMA((n_dp,)),
            pltpu.SemaphoreType.DMA((n_dp,)),
        ],
        compiler_params=pltpu.CompilerParams(
            collective_id=0, has_side_effects=True, vmem_limit_bytes=44 * 1024 * 1024
        ),
        cost_estimate=pl.CostEstimate(
            flops=4 * xt.shape[0] * depth * hidden, bytes_accessed=1 << 24, transcendentals=0
        ),
        name="grad_sums",
    )(xt, ct, dh, act, boxed)


def part_orders(bits):
    group, near, next_near = bits - 1, bits - 2, bits - 3
    rest = [bit for bit in range(bits - 4, -1, -1)]
    return [
        [near, group, next_near] + rest,
        [group, near, next_near] + rest,
        [next_near, group, near] + rest,
    ]


def local(
    ref_image,
    ref_text,
    learner_image,
    learner_text,
    patches,
    cotangent,
    w_up,
    w_down,
    counts,
    sel_index,
    sel_dest,
):
    tensor_at = lax.axis_index("tensor")
    dp_at = lax.axis_index("dp")
    n_dp = lax.axis_size("dp")
    slots = sel_index.shape[0]
    cap = max(2, 2 * slots // n_dp)
    patch_rows, half_width = (patches.shape[1], patches.shape[2])
    count = slots * patch_rows
    half_x = patches[sel_index].reshape(count, half_width)
    half_cot = cotangent[sel_index].reshape(count, half_width)

    scores, other_x, other_cot = shard_learnability(
        ref_image, ref_text, learner_image, learner_text, half_x, half_cot, n_dp
    )

    def widen(half, other):
        return jnp.concatenate(
            [jnp.where(tensor_at == 0, half, other), jnp.where(tensor_at == 0, other, half)], axis=1
        )

    x = widen(half_x, other_x)
    cot = widen(half_cot, other_cot)
    pre = jnp.dot(x, w_up, preferred_element_type=jnp.float32)
    act_full, gelu_back = jax.vjp(jax.nn.gelu, pre)
    act = lax.optimization_barrier(act_full.astype(jnp.bfloat16))
    def down(side):
        columns = lax.dynamic_slice_in_dim(w_down, side * half_width, half_width, 1)
        return jnp.dot(act, columns, preferred_element_type=jnp.float32)

    came = swap(down(1 - tensor_at).astype(jnp.bfloat16), ("tensor",), (1,))
    out = (half_x.astype(jnp.float32) + (down(tensor_at) + came.astype(jnp.float32))).astype(
        jnp.bfloat16
    )
    back = jnp.einsum("md,fd->mf", cot, w_down, preferred_element_type=jnp.float32)
    grad_pre = lax.optimization_barrier(gelu_back(back)[0])

    live = jnp.arange(slots, dtype=jnp.int32) < counts[0]
    target = sel_dest[:, 0]
    earlier = jnp.arange(slots)[:, None] > jnp.arange(slots)[None, :]
    rank = jnp.sum(
        (earlier & (target[:, None] == target[None, :]) & live[None, :]).astype(jnp.int32), axis=1
    )
    bucket = (target ^ dp_at) * cap + rank
    slot_row = jnp.repeat(jnp.where(live, bucket, -1), patch_rows) * patch_rows + jnp.tile(
        jnp.arange(patch_rows, dtype=jnp.int32), slots
    )
    placer = (
        jnp.arange(n_dp * cap * patch_rows, dtype=jnp.int32)[:, None] == slot_row[None, :]
    ).astype(jnp.bfloat16)
    boxed = jnp.dot(placer, out, preferred_element_type=jnp.float32).astype(jnp.bfloat16)
    boxed = boxed.reshape(n_dp, cap * patch_rows, half_width)

    pairs = learner_image.shape[0]
    learnability = scores[0, 0, :pairs]
    other_scores = scores[1, 0, :pairs]
    shard_scores = jnp.concatenate(
        [
            jnp.where(tensor_at == 0, learnability, other_scores),
            jnp.where(tensor_at == 0, other_scores, learnability),
        ]
    )
    picked = sel_index[:, None] == jnp.arange(patches.shape[0], dtype=jnp.int32)[None, :]
    score_sel = jnp.sum(jnp.where(picked, shard_scores[None, :], 0.0), axis=1)
    weight = jnp.where(live, jax.nn.sigmoid(score_sel), 0.0)
    row_weight = jnp.repeat(weight, patch_rows)[:, None]

    axis_bits = [("dp", 1 << bit) for bit in range(n_dp.bit_length() - 2, -1, -1)] + [("group", 1)]
    dh = (row_weight * grad_pre).astype(jnp.bfloat16)
    weighted_act = (row_weight * act.astype(jnp.float32)).astype(jnp.bfloat16)
    grad_up, grad_down_t, landed = gradients(
        x.T, cot.T, dh, weighted_act, boxed, axis_bits
    )
    routed = landed.reshape(n_dp * cap, patch_rows, half_width)
    return (learnability, routed, grad_up, grad_down_t)


def solution(mesh):
    placed = (
        P(("dp", "tensor"), None),
        P(("dp", "tensor"), None),
        P(("dp", "tensor"), None),
        P(("dp", "tensor"), None),
        P("dp", "group", "tensor"),
        P("dp", "group", "tensor"),
        P(None, "tensor"),
        P("tensor", None),
        P("dp"),
        P("dp"),
        P("dp", None),
    )
    return jax.shard_map(
        local,
        mesh=mesh,
        in_specs=placed,
        out_specs=(
            P(("dp", "tensor")),
            P("dp", "group", "tensor"),
            P(("dp", "group"), "tensor"),
            P(("dp", "group"), "tensor"),
        ),
        check_vma=False,
    )
```

```python
import itertools
import jax
import jax.numpy as jnp
from jax import lax
from jax.experimental import pallas as pl
from jax.experimental.pallas import tpu as pltpu
from jax.sharding import PartitionSpec as P


def swap(block, axes, mask):
    names = tuple(axes)
    sizes = [lax.axis_size(name) for name in names]
    total = 1
    for size in sizes:
        total *= size
    route = []
    for start in range(total):
        rest, end, scale = start, 0, 1
        for size, bits in zip(reversed(sizes), reversed(mask)):
            end += ((rest % size) ^ bits) * scale
            rest //= size
            scale *= size
        route.append((start, end))
    return lax.ppermute(block, names if len(names) > 1 else names[0], route)


def flip(index, mask):
    out, bit = index, 1
    while bit <= mask:
        if mask & bit:
            out = out + bit * (1 - 2 * ((index // bit) % 2))
        bit *= 2
    return out


def loss_kernel(
    n_dp, temp, bias,
    ref_img, ref_txt, own_img, own_txt, half_x, half_cot, up_ref, down_ref,
    score_ref, wide_x, wide_cot, act_ref, grad_pre_ref,
    imgs, txts, row_out, row_in, text_out, text_in, share, share_in, send_sem, recv_sem,
):
    rows, width = own_img.shape
    far = n_dp // 2
    dp_at, tensor_at = lax.axis_index("dp"), lax.axis_index("tensor")
    group_at = lax.axis_index("group")
    over_tensor = {"tensor": 1 - tensor_at}
    near = [
        over_tensor,
        {"dp": flip(dp_at, 1)},
        {"dp": flip(dp_at, 1), "tensor": 1 - tensor_at},
    ]
    across = [{"dp": flip(dp_at, 2 * mask)} for mask in range(1, far)]
    models = [{"group": 1 - group_at}, {"group": 1 - group_at, "tensor": 1 - tensor_at}]
    partners = near + across + models
    barrier = pltpu.get_barrier_semaphore()
    for partner in partners:
        pl.semaphore_signal(
            barrier, inc=1, device_id=partner, device_id_type=pl.DeviceIdType.MESH
        )

    def put(value, dest):
        wide = value[...].astype(jnp.float32)
        total = jnp.sum(wide * wide, axis=1, keepdims=True)
        dest[:, : value.shape[1]] = (wide * lax.rsqrt(total + 1e-06)).astype(jnp.bfloat16)

    @pl.when(group_at == 0)
    def _():
        for raw, dest in ((ref_img, imgs.at[0]), (ref_txt, txts.at[0])):
            dest[...] = jnp.zeros((rows, width), jnp.bfloat16)
            put(raw, dest)

    @pl.when(group_at == 1)
    def _():
        put(own_img, imgs.at[0])
        put(own_txt, txts.at[0])

    pl.semaphore_wait(barrier, len(partners))
    used = [0]

    def send(src, dest, partner):
        at = used[0]
        used[0] += 1
        copy = pltpu.make_async_remote_copy(
            src_ref=src,
            dst_ref=dest,
            send_sem=send_sem.at[at],
            recv_sem=recv_sem.at[at],
            device_id=partner,
            device_id_type=pl.DeviceIdType.MESH,
        )
        copy.start()
        return copy

    copies = [send(txts.at[0], txts.at[m], to) for m, to in enumerate(across, 1)]
    copies += [send(imgs.at[0], imgs.at[m], to) for m, to in enumerate(near, 1)]
    half_width = half_x.shape[1]
    columns = pl.ds(pl.multiple_of(tensor_at * half_width, half_width), half_width)
    wide_copies = [
        send(half_x, wide_x.at[:, columns], over_tensor),
        send(half_cot, wide_cot.at[:, columns], over_tensor),
    ]
    wide_x[:, columns] = half_x[...]
    wide_cot[:, columns] = half_cot[...]
    for copy in wide_copies:
        copy.wait()

    def forward(step, carry):
        tile = pl.ds(pl.multiple_of(step * 256, 256), 256)
        h = jnp.dot(wide_x[...], up_ref[:, tile], preferred_element_type=jnp.float32)
        back = lax.dot_general(
            wide_cot[...], down_ref[tile, :], (((1,), (1,)), ((), ())),
            preferred_element_type=jnp.float32,
        )
        slope = 0.7978845608028654
        square = h * h
        bend = jnp.tanh(slope * h * (1.0 + 0.044715 * square))
        cdf = 0.5 * (1.0 + bend)
        act_ref[:, tile] = (h * cdf).astype(jnp.bfloat16)
        rise = cdf + 0.5 * h * (1.0 - bend * bend) * (slope * (1.0 + 0.134145 * square))
        grad_pre_ref[:, tile] = (back * rise).astype(jnp.bfloat16)
        return carry

    lax.fori_loop(0, up_ref.shape[1] // 256, forward, 0)
    for copy in copies:
        copy.wait()

    def sums(long, short, has_own):
        scores = temp * lax.dot_general(
            long, short, (((1,), (1,)), ((), ())), preferred_element_type=jnp.float32
        ) + bias
        if has_own:
            at_row = lax.broadcasted_iota(jnp.int32, scores.shape, 0)
            at_col = lax.broadcasted_iota(jnp.int32, scores.shape, 1)
            scores = jnp.where(at_row == at_col, -scores, scores)
        terms = jnp.maximum(scores, 0.0) + jnp.log1p(jnp.exp(-jnp.abs(scores)))
        total = jnp.sum(terms, axis=0, keepdims=True)
        total = jnp.concatenate([total, jnp.zeros((1, 128 - rows), jnp.float32)], axis=1)
        return jnp.broadcast_to(total, (8, 128))

    all_txt = txts[...].reshape(far * rows, width)
    all_img = imgs[...].reshape(4 * rows, width)
    by_image = [sums(all_txt, imgs[m], m == 0) for m in range(4)]
    row_out[0] = by_image[2]
    row_out[1] = by_image[3]
    copies = [send(row_out, row_in, near[1])]
    for m in range(1, far):
        text_out[m] = sums(all_img, txts[m], False)
        copies.append(send(text_out.at[m], text_in.at[m], across[m - 1]))
    own_text = sums(all_img, txts[0], True)
    for copy in copies:
        copy.wait()
    for m in range(1, far):
        own_text = own_text + text_in[m]
    share[0] = 0.5 * (by_image[0] + row_in[0] + own_text)
    share[1] = 0.5 * (by_image[1] + row_in[1])
    copies = [
        send(share, share_in.at[m], to) for m, to in enumerate([over_tensor] + models)
    ]
    for copy in copies:
        copy.wait()
    for half in range(2):
        mine = share[half] + share_in[0, 1 - half]
        partner = share_in[1, half] + share_in[2, 1 - half]
        score_ref[half] = jnp.where(group_at == 0, partner - mine, mine - partner)


def shard_learnability(
    ref_img, ref_txt, own_img, own_txt, half_x, half_cot, w_up, w_down, n_dp
):
    rows, width = own_img.shape
    far = n_dp // 2
    copies = 3 + (far - 1) + 2 + 1 + (far - 1) + 3
    vmem = pl.BlockSpec(memory_space=pltpu.VMEM)
    kernel = lambda *refs: loss_kernel(n_dp, 10.0, -5.0, *refs)
    tile = (8, 128)
    return pl.pallas_call(
        kernel,
        out_shape=(
            jax.ShapeDtypeStruct((2,) + tile, jnp.float32),
            jax.ShapeDtypeStruct((half_x.shape[0], w_up.shape[0]), half_x.dtype),
            jax.ShapeDtypeStruct((half_x.shape[0], w_up.shape[0]), half_x.dtype),
            jax.ShapeDtypeStruct((half_x.shape[0], w_up.shape[1]), jnp.bfloat16),
            jax.ShapeDtypeStruct((half_x.shape[0], w_up.shape[1]), jnp.bfloat16),
        ),
        in_specs=[vmem] * 8,
        out_specs=(vmem,) * 5,
        scratch_shapes=[
            pltpu.VMEM((4, rows, width), jnp.bfloat16),
            pltpu.VMEM((far, rows, width), jnp.bfloat16),
            pltpu.VMEM((2,) + tile, jnp.float32),
            pltpu.VMEM((2,) + tile, jnp.float32),
            pltpu.VMEM((far,) + tile, jnp.float32),
            pltpu.VMEM((far,) + tile, jnp.float32),
            pltpu.VMEM((2,) + tile, jnp.float32),
            pltpu.VMEM((3, 2) + tile, jnp.float32),
            pltpu.SemaphoreType.DMA((copies,)),
            pltpu.SemaphoreType.DMA((copies,)),
        ],
        compiler_params=pltpu.CompilerParams(
            collective_id=1, has_side_effects=True, vmem_limit_bytes=16 * 1024 * 1024
        ),
        cost_estimate=pl.CostEstimate(
            flops=16 * rows * rows * far * width, bytes_accessed=1 << 22, transcendentals=1 << 18
        ),
        name="pair_losses",
    )(ref_img, ref_txt, own_img, own_txt, half_x, half_cot, w_up, w_down)


def grad_kernel(
    axis_bits, orders, widths, subs, n_dp,
    xt_ref, ct_ref, dh_ref, act_ref, boxed_ref,
    up_ref, down_ref, landed_ref,
    *scratch,
):
    bits, kinds = len(axis_bits), len(orders)
    prods = scratch[:kinds]
    recvs = [scratch[kinds + kind * bits : kinds + (kind + 1) * bits] for kind in range(kinds)]
    send_sem, recv_sem, box_send, box_recv = scratch[kinds + kinds * bits :]
    dp_at = lax.axis_index("dp")
    group_at = lax.axis_index("group")
    at = {"dp": dp_at, "group": group_at}

    barrier = pltpu.get_barrier_semaphore()
    partners = [{"dp": flip(dp_at, mask)} for mask in range(1, n_dp)]
    partners.append({"group": 1 - group_at})
    for partner in partners:
        pl.semaphore_signal(
            barrier, inc=1, device_id=partner, device_id_type=pl.DeviceIdType.MESH
        )
    pl.semaphore_wait(barrier, len(partners))

    def pick(ref, lead, left, bit, value):
        place = [slice(None)] * len(left)
        place[left.index(bit)] = value
        return ref.at[tuple(lead + place)]

    def source(kind, step):
        return prods[kind] if step == 0 else recvs[kind][step - 1]

    def exchange(kind, turn, step):
        bit = orders[kind][step]
        left = [other for other in range(bits) if other not in orders[kind][:step]]
        name, mask = axis_bits[bit]
        mine = (at[name] // mask) % 2
        ref = source(kind, step)
        copy = pltpu.make_async_remote_copy(
            src_ref=pick(ref, [turn], left, bit, 1 - mine),
            dst_ref=recvs[kind][step].at[turn],
            send_sem=send_sem.at[kind, turn, step],
            recv_sem=recv_sem.at[kind, turn, step],
            device_id={name: flip(at[name], mask)},
            device_id_type=pl.DeviceIdType.MESH,
        )
        return copy, pick(ref, [turn], left, bit, mine)

    turns = 2 * subs
    starts = [subs * sum(widths[:kind]) for kind in range(kinds)]
    flight = {}
    for turn in range(turns):
        rows_ref, cols_ref = ((xt_ref, dh_ref), (ct_ref, act_ref))[turn // subs]
        for kind in range(kinds):
            width = widths[kind]
            low = starts[kind] + (turn % subs) * width
            tile = rows_ref.shape[0] // 4

            def multiply(tile_at, carry, kind=kind, turn=turn, low=low, width=width,
                         rows_ref=rows_ref, cols_ref=cols_ref, tile=tile):
                product = jnp.dot(
                    rows_ref[pl.ds(pl.multiple_of(tile_at * tile, tile), tile), :],
                    cols_ref[:, low : low + width],
                    preferred_element_type=jnp.float32,
                )
                dest = prods[kind].at[turn, tile_at // 2, tile_at % 2]
                dest[...] = product.astype(jnp.bfloat16).reshape(dest.shape)
                return carry

            lax.fori_loop(0, 4, multiply, 0)
            copy, keep = exchange(kind, turn, 0)
            copy.start()
            flight[kind, turn] = (copy, keep)

    boxes = []
    for mask in range(1, n_dp):
        box = pltpu.make_async_remote_copy(
            src_ref=boxed_ref.at[mask],
            dst_ref=landed_ref.at[dp_at],
            send_sem=box_send.at[mask],
            recv_sem=box_recv.at[mask],
            device_id={"dp": flip(dp_at, mask)},
            device_id_type=pl.DeviceIdType.MESH,
        )
        box.start()
        boxes.append(box)
    landed_ref[dp_at] = boxed_ref[0]

    sent = []
    for step in range(bits):
        for turn in range(turns):
            for kind in range(kinds):
                copy, keep = flight[kind, turn]
                copy.wait_recv()
                sent.append(copy)
                came = recvs[kind][step].at[turn]
                if step < bits - 1:
                    for lead in itertools.product(*[range(size) for size in came.shape[:-2]]):
                        came[lead] = (
                            came[lead].astype(jnp.float32) + keep[lead].astype(jnp.float32)
                        ).astype(jnp.bfloat16)
                    copy, keep = exchange(kind, turn, step + 1)
                    copy.start()
                    flight[kind, turn] = (copy, keep)
                else:
                    out_ref = (up_ref, down_ref)[turn // subs]
                    low = starts[kind] + (turn % subs) * widths[kind]
                    out_ref[:, low : low + widths[kind]] = came[...].astype(jnp.float32) + keep[
                        ...
                    ].astype(jnp.float32)
    for copy in sent:
        copy.wait_send()
    for box in boxes:
        box.wait()


def gradients(xt, ct, dh, act, boxed, axis_bits):
    bits = len(axis_bits)
    orders = part_orders(bits)
    depth, hidden = dh.shape
    subs = 2
    widths = [hidden * 3 // 8 // subs, hidden * 3 // 8 // subs, hidden // 4 // subs]
    turns = 2 * subs
    rows = xt.shape[0] >> bits
    n_dp = boxed.shape[0]
    prods = [
        pltpu.VMEM((turns,) + (2,) * bits + (rows, width), jnp.bfloat16) for width in widths
    ]
    recvs = [
        pltpu.VMEM((turns,) + (2,) * (bits - 1 - step) + (rows, width), jnp.bfloat16)
        for width in widths
        for step in range(bits)
    ]
    vmem = pl.BlockSpec(memory_space=pltpu.VMEM)
    kernel = lambda *refs: grad_kernel(axis_bits, orders, widths, subs, n_dp, *refs)
    return pl.pallas_call(
        kernel,
        out_shape=(
            jax.ShapeDtypeStruct((rows, hidden), jnp.float32),
            jax.ShapeDtypeStruct((rows, hidden), jnp.float32),
            jax.ShapeDtypeStruct(boxed.shape, boxed.dtype),
        ),
        in_specs=[vmem] * 5,
        out_specs=(vmem, vmem, vmem),
        scratch_shapes=prods
        + recvs
        + [
            pltpu.SemaphoreType.DMA((len(orders), turns, bits)),
            pltpu.SemaphoreType.DMA((len(orders), turns, bits)),
            pltpu.SemaphoreType.DMA((n_dp,)),
            pltpu.SemaphoreType.DMA((n_dp,)),
        ],
        compiler_params=pltpu.CompilerParams(
            collective_id=0, has_side_effects=True, vmem_limit_bytes=24 * 1024 * 1024
        ),
        cost_estimate=pl.CostEstimate(
            flops=4 * xt.shape[0] * depth * hidden, bytes_accessed=1 << 24, transcendentals=0
        ),
        name="grad_sums",
    )(xt, ct, dh, act, boxed)


def part_orders(bits):
    group, near, next_near = bits - 1, bits - 2, bits - 3
    rest = [bit for bit in range(bits - 4, -1, -1)]
    return [
        [near, group, next_near] + rest,
        [group, near, next_near] + rest,
        [next_near, group, near] + rest,
    ]


def local(
    ref_image,
    ref_text,
    learner_image,
    learner_text,
    patches,
    cotangent,
    w_up,
    w_down,
    counts,
    sel_index,
    sel_dest,
):
    tensor_at = lax.axis_index("tensor")
    dp_at = lax.axis_index("dp")
    n_dp = lax.axis_size("dp")
    slots = sel_index.shape[0]
    cap = max(2, 2 * slots // n_dp)
    patch_rows, half_width = (patches.shape[1], patches.shape[2])
    count = slots * patch_rows
    half_x = patches[sel_index].reshape(count, half_width)
    half_cot = cotangent[sel_index].reshape(count, half_width)

    scores, x, cot, act, grad_pre = shard_learnability(
        ref_image, ref_text, learner_image, learner_text, half_x, half_cot, w_up, w_down, n_dp
    )

    def down(side):
        columns = lax.dynamic_slice_in_dim(w_down, side * half_width, half_width, 1)
        return jnp.dot(act, columns, preferred_element_type=jnp.float32)

    came = swap(down(1 - tensor_at).astype(jnp.bfloat16), ("tensor",), (1,))
    out = (half_x.astype(jnp.float32) + (down(tensor_at) + came.astype(jnp.float32))).astype(
        jnp.bfloat16
    )
    live = jnp.arange(slots, dtype=jnp.int32) < counts[0]
    target = sel_dest[:, 0]
    earlier = jnp.arange(slots)[:, None] > jnp.arange(slots)[None, :]
    rank = jnp.sum(
        (earlier & (target[:, None] == target[None, :]) & live[None, :]).astype(jnp.int32), axis=1
    )
    bucket = (target ^ dp_at) * cap + rank
    slot_row = jnp.repeat(jnp.where(live, bucket, -1), patch_rows) * patch_rows + jnp.tile(
        jnp.arange(patch_rows, dtype=jnp.int32), slots
    )
    placer = (
        jnp.arange(n_dp * cap * patch_rows, dtype=jnp.int32)[:, None] == slot_row[None, :]
    ).astype(jnp.bfloat16)
    boxed = jnp.dot(placer, out, preferred_element_type=jnp.float32).astype(jnp.bfloat16)
    boxed = boxed.reshape(n_dp, cap * patch_rows, half_width)

    pairs = learner_image.shape[0]
    learnability = scores[0, 0, :pairs]
    other_scores = scores[1, 0, :pairs]
    shard_scores = jnp.concatenate(
        [
            jnp.where(tensor_at == 0, learnability, other_scores),
            jnp.where(tensor_at == 0, other_scores, learnability),
        ]
    )
    picked = sel_index[:, None] == jnp.arange(patches.shape[0], dtype=jnp.int32)[None, :]
    score_sel = jnp.sum(jnp.where(picked, shard_scores[None, :], 0.0), axis=1)
    weight = jnp.where(live, jax.nn.sigmoid(score_sel), 0.0)
    row_weight = jnp.repeat(weight, patch_rows)[:, None]

    axis_bits = [("dp", 1 << bit) for bit in range(n_dp.bit_length() - 2, -1, -1)] + [("group", 1)]
    dh = (row_weight * grad_pre.astype(jnp.float32)).astype(jnp.bfloat16)
    weighted_act = (row_weight * act.astype(jnp.float32)).astype(jnp.bfloat16)
    grad_up, grad_down_t, landed = gradients(
        x.T, cot.T, dh, weighted_act, boxed, axis_bits
    )
    routed = landed.reshape(n_dp * cap, patch_rows, half_width)
    return (learnability, routed, grad_up, grad_down_t)


def solution(mesh):
    placed = (
        P(("dp", "tensor"), None),
        P(("dp", "tensor"), None),
        P(("dp", "tensor"), None),
        P(("dp", "tensor"), None),
        P("dp", "group", "tensor"),
        P("dp", "group", "tensor"),
        P(None, "tensor"),
        P("tensor", None),
        P("dp"),
        P("dp"),
        P("dp", None),
    )
    return jax.shard_map(
        local,
        mesh=mesh,
        in_specs=placed,
        out_specs=(
            P(("dp", "tensor")),
            P("dp", "group", "tensor"),
            P(("dp", "group"), "tensor"),
            P(("dp", "group"), "tensor"),
        ),
        check_vma=False,
    )
```

```python
import itertools
import jax
import jax.numpy as jnp
from jax import lax
from jax.experimental import pallas as pl
from jax.experimental.pallas import tpu as pltpu
from jax.sharding import PartitionSpec as P


def swap(block, axes, mask):
    names = tuple(axes)
    sizes = [lax.axis_size(name) for name in names]
    total = 1
    for size in sizes:
        total *= size
    route = []
    for start in range(total):
        rest, end, scale = start, 0, 1
        for size, bits in zip(reversed(sizes), reversed(mask)):
            end += ((rest % size) ^ bits) * scale
            rest //= size
            scale *= size
        route.append((start, end))
    return lax.ppermute(block, names if len(names) > 1 else names[0], route)


def flip(index, mask):
    out, bit = index, 1
    while bit <= mask:
        if mask & bit:
            out = out + bit * (1 - 2 * ((index // bit) % 2))
        bit *= 2
    return out


def loss_kernel(
    n_dp, temp, bias,
    ref_img, ref_txt, own_img, own_txt, half_x, half_cot, up_ref, down_ref,
    score_ref, xt_ref, ct_ref, act_ref, grad_pre_ref,
    wide_x, wide_cot, imgs, txts, row_out, row_in, text_out, text_in, share, share_in, send_sem, recv_sem,
):
    rows, width = own_img.shape
    far = n_dp // 2
    dp_at, tensor_at = lax.axis_index("dp"), lax.axis_index("tensor")
    group_at = lax.axis_index("group")
    over_tensor = {"tensor": 1 - tensor_at}
    near = [
        over_tensor,
        {"dp": flip(dp_at, 1)},
        {"dp": flip(dp_at, 1), "tensor": 1 - tensor_at},
    ]
    across = [{"dp": flip(dp_at, 2 * mask)} for mask in range(1, far)]
    models = [{"group": 1 - group_at}, {"group": 1 - group_at, "tensor": 1 - tensor_at}]
    partners = near + across + models
    barrier = pltpu.get_barrier_semaphore()
    for partner in partners:
        pl.semaphore_signal(
            barrier, inc=1, device_id=partner, device_id_type=pl.DeviceIdType.MESH
        )

    def put(value, dest):
        wide = value[...].astype(jnp.float32)
        total = jnp.sum(wide * wide, axis=1, keepdims=True)
        dest[:, : value.shape[1]] = (wide * lax.rsqrt(total + 1e-06)).astype(jnp.bfloat16)

    @pl.when(group_at == 0)
    def _():
        for raw, dest in ((ref_img, imgs.at[0]), (ref_txt, txts.at[0])):
            dest[...] = jnp.zeros((rows, width), jnp.bfloat16)
            put(raw, dest)

    @pl.when(group_at == 1)
    def _():
        put(own_img, imgs.at[0])
        put(own_txt, txts.at[0])

    pl.semaphore_wait(barrier, len(partners))
    used = [0]

    def send(src, dest, partner):
        at = used[0]
        used[0] += 1
        copy = pltpu.make_async_remote_copy(
            src_ref=src,
            dst_ref=dest,
            send_sem=send_sem.at[at],
            recv_sem=recv_sem.at[at],
            device_id=partner,
            device_id_type=pl.DeviceIdType.MESH,
        )
        copy.start()
        return copy

    copies = [send(txts.at[0], txts.at[m], to) for m, to in enumerate(across, 1)]
    copies += [send(imgs.at[0], imgs.at[m], to) for m, to in enumerate(near, 1)]
    half_width = half_x.shape[1]
    columns = pl.ds(pl.multiple_of(tensor_at * half_width, half_width), half_width)
    wide_copies = [
        send(half_x, wide_x.at[:, columns], over_tensor),
        send(half_cot, wide_cot.at[:, columns], over_tensor),
    ]
    wide_x[:, columns] = half_x[...]
    wide_cot[:, columns] = half_cot[...]
    for copy in wide_copies:
        copy.wait()

    def forward(step, carry):
        tile = pl.ds(pl.multiple_of(step * 256, 256), 256)
        h = jnp.dot(wide_x[...], up_ref[:, tile], preferred_element_type=jnp.float32)
        back = lax.dot_general(
            wide_cot[...], down_ref[tile, :], (((1,), (1,)), ((), ())),
            preferred_element_type=jnp.float32,
        )
        slope = 0.7978845608028654
        square = h * h
        bend = jnp.tanh(slope * h * (1.0 + 0.044715 * square))
        cdf = 0.5 * (1.0 + bend)
        act_ref[:, tile] = (h * cdf).astype(jnp.bfloat16)
        rise = cdf + 0.5 * h * (1.0 - bend * bend) * (slope * (1.0 + 0.134145 * square))
        grad_pre_ref[:, tile] = (back * rise).astype(jnp.bfloat16)
        return carry

    lax.fori_loop(0, up_ref.shape[1] // 256, forward, 0)
    xt_ref[...] = wide_x[...].T
    ct_ref[...] = wide_cot[...].T
    for copy in copies:
        copy.wait()

    def sums(long, short, has_own):
        scores = temp * lax.dot_general(
            long, short, (((1,), (1,)), ((), ())), preferred_element_type=jnp.float32
        ) + bias
        if has_own:
            at_row = lax.broadcasted_iota(jnp.int32, scores.shape, 0)
            at_col = lax.broadcasted_iota(jnp.int32, scores.shape, 1)
            scores = jnp.where(at_row == at_col, -scores, scores)
        terms = jnp.maximum(scores, 0.0) + jnp.log1p(jnp.exp(-jnp.abs(scores)))
        total = jnp.sum(terms, axis=0, keepdims=True)
        total = jnp.concatenate([total, jnp.zeros((1, 128 - rows), jnp.float32)], axis=1)
        return jnp.broadcast_to(total, (8, 128))

    all_txt = txts[...].reshape(far * rows, width)
    all_img = imgs[...].reshape(4 * rows, width)
    by_image = [sums(all_txt, imgs[m], m == 0) for m in range(4)]
    row_out[0] = by_image[2]
    row_out[1] = by_image[3]
    copies = [send(row_out, row_in, near[1])]
    for m in range(1, far):
        text_out[m] = sums(all_img, txts[m], False)
        copies.append(send(text_out.at[m], text_in.at[m], across[m - 1]))
    own_text = sums(all_img, txts[0], True)
    for copy in copies:
        copy.wait()
    for m in range(1, far):
        own_text = own_text + text_in[m]
    share[0] = 0.5 * (by_image[0] + row_in[0] + own_text)
    share[1] = 0.5 * (by_image[1] + row_in[1])
    copies = [
        send(share, share_in.at[m], to) for m, to in enumerate([over_tensor] + models)
    ]
    for copy in copies:
        copy.wait()
    for half in range(2):
        mine = share[half] + share_in[0, 1 - half]
        partner = share_in[1, half] + share_in[2, 1 - half]
        score_ref[half] = jnp.where(group_at == 0, partner - mine, mine - partner)


def shard_learnability(
    ref_img, ref_txt, own_img, own_txt, half_x, half_cot, w_up, w_down, n_dp
):
    rows, width = own_img.shape
    far = n_dp // 2
    copies = 3 + (far - 1) + 2 + 1 + (far - 1) + 3
    vmem = pl.BlockSpec(memory_space=pltpu.VMEM)
    kernel = lambda *refs: loss_kernel(n_dp, 10.0, -5.0, *refs)
    tile = (8, 128)
    return pl.pallas_call(
        kernel,
        out_shape=(
            jax.ShapeDtypeStruct((2,) + tile, jnp.float32),
            jax.ShapeDtypeStruct((w_up.shape[0], half_x.shape[0]), half_x.dtype),
            jax.ShapeDtypeStruct((w_up.shape[0], half_x.shape[0]), half_x.dtype),
            jax.ShapeDtypeStruct((half_x.shape[0], w_up.shape[1]), jnp.bfloat16),
            jax.ShapeDtypeStruct((half_x.shape[0], w_up.shape[1]), jnp.bfloat16),
        ),
        in_specs=[vmem] * 8,
        out_specs=(vmem,) * 5,
        scratch_shapes=[
            pltpu.VMEM((half_x.shape[0], w_up.shape[0]), jnp.bfloat16),
            pltpu.VMEM((half_x.shape[0], w_up.shape[0]), jnp.bfloat16),
            pltpu.VMEM((4, rows, width), jnp.bfloat16),
            pltpu.VMEM((far, rows, width), jnp.bfloat16),
            pltpu.VMEM((2,) + tile, jnp.float32),
            pltpu.VMEM((2,) + tile, jnp.float32),
            pltpu.VMEM((far,) + tile, jnp.float32),
            pltpu.VMEM((far,) + tile, jnp.float32),
            pltpu.VMEM((2,) + tile, jnp.float32),
            pltpu.VMEM((3, 2) + tile, jnp.float32),
            pltpu.SemaphoreType.DMA((copies,)),
            pltpu.SemaphoreType.DMA((copies,)),
        ],
        compiler_params=pltpu.CompilerParams(
            collective_id=1, has_side_effects=True, vmem_limit_bytes=16 * 1024 * 1024
        ),
        cost_estimate=pl.CostEstimate(
            flops=16 * rows * rows * far * width, bytes_accessed=1 << 22, transcendentals=1 << 18
        ),
        name="pair_losses",
    )(ref_img, ref_txt, own_img, own_txt, half_x, half_cot, w_up, w_down)


def grad_kernel(
    axis_bits, orders, widths, subs, n_dp,
    xt_ref, ct_ref, dh_ref, act_ref, boxed_ref,
    up_ref, down_ref, landed_ref,
    *scratch,
):
    bits, kinds = len(axis_bits), len(orders)
    prods = scratch[:kinds]
    recvs = [scratch[kinds + kind * bits : kinds + (kind + 1) * bits] for kind in range(kinds)]
    send_sem, recv_sem, box_send, box_recv = scratch[kinds + kinds * bits :]
    dp_at = lax.axis_index("dp")
    group_at = lax.axis_index("group")
    at = {"dp": dp_at, "group": group_at}

    barrier = pltpu.get_barrier_semaphore()
    partners = [{"dp": flip(dp_at, mask)} for mask in range(1, n_dp)]
    partners.append({"group": 1 - group_at})
    for partner in partners:
        pl.semaphore_signal(
            barrier, inc=1, device_id=partner, device_id_type=pl.DeviceIdType.MESH
        )
    pl.semaphore_wait(barrier, len(partners))

    def pick(ref, lead, left, bit, value):
        place = [slice(None)] * len(left)
        place[left.index(bit)] = value
        return ref.at[tuple(lead + place)]

    def source(kind, step):
        return prods[kind] if step == 0 else recvs[kind][step - 1]

    def exchange(kind, turn, step):
        bit = orders[kind][step]
        left = [other for other in range(bits) if other not in orders[kind][:step]]
        name, mask = axis_bits[bit]
        mine = (at[name] // mask) % 2
        ref = source(kind, step)
        copy = pltpu.make_async_remote_copy(
            src_ref=pick(ref, [turn], left, bit, 1 - mine),
            dst_ref=recvs[kind][step].at[turn],
            send_sem=send_sem.at[kind, turn, step],
            recv_sem=recv_sem.at[kind, turn, step],
            device_id={name: flip(at[name], mask)},
            device_id_type=pl.DeviceIdType.MESH,
        )
        return copy, pick(ref, [turn], left, bit, mine)

    turns = 2 * subs
    starts = [subs * sum(widths[:kind]) for kind in range(kinds)]
    flight = {}
    for turn in range(turns):
        rows_ref, cols_ref = ((xt_ref, dh_ref), (ct_ref, act_ref))[turn // subs]
        for kind in range(kinds):
            width = widths[kind]
            low = starts[kind] + (turn % subs) * width
            tile = rows_ref.shape[0] // 4

            def multiply(tile_at, carry, kind=kind, turn=turn, low=low, width=width,
                         rows_ref=rows_ref, cols_ref=cols_ref, tile=tile):
                product = jnp.dot(
                    rows_ref[pl.ds(pl.multiple_of(tile_at * tile, tile), tile), :],
                    cols_ref[:, low : low + width],
                    preferred_element_type=jnp.float32,
                )
                dest = prods[kind].at[turn, tile_at // 2, tile_at % 2]
                dest[...] = product.astype(jnp.bfloat16).reshape(dest.shape)
                return carry

            lax.fori_loop(0, 4, multiply, 0)
            copy, keep = exchange(kind, turn, 0)
            copy.start()
            flight[kind, turn] = (copy, keep)

    boxes = []
    for mask in range(1, n_dp):
        box = pltpu.make_async_remote_copy(
            src_ref=boxed_ref.at[mask],
            dst_ref=landed_ref.at[dp_at],
            send_sem=box_send.at[mask],
            recv_sem=box_recv.at[mask],
            device_id={"dp": flip(dp_at, mask)},
            device_id_type=pl.DeviceIdType.MESH,
        )
        box.start()
        boxes.append(box)
    landed_ref[dp_at] = boxed_ref[0]

    sent = []
    for step in range(bits):
        for turn in range(turns):
            for kind in range(kinds):
                copy, keep = flight[kind, turn]
                copy.wait_recv()
                sent.append(copy)
                came = recvs[kind][step].at[turn]
                if step < bits - 1:
                    for lead in itertools.product(*[range(size) for size in came.shape[:-2]]):
                        came[lead] = (
                            came[lead].astype(jnp.float32) + keep[lead].astype(jnp.float32)
                        ).astype(jnp.bfloat16)
                    copy, keep = exchange(kind, turn, step + 1)
                    copy.start()
                    flight[kind, turn] = (copy, keep)
                else:
                    out_ref = (up_ref, down_ref)[turn // subs]
                    low = starts[kind] + (turn % subs) * widths[kind]
                    out_ref[:, low : low + widths[kind]] = came[...].astype(jnp.float32) + keep[
                        ...
                    ].astype(jnp.float32)
    for copy in sent:
        copy.wait_send()
    for box in boxes:
        box.wait()


def gradients(xt, ct, dh, act, boxed, axis_bits):
    bits = len(axis_bits)
    orders = part_orders(bits)
    depth, hidden = dh.shape
    subs = 2
    widths = [hidden * 3 // 8 // subs, hidden * 3 // 8 // subs, hidden // 4 // subs]
    turns = 2 * subs
    rows = xt.shape[0] >> bits
    n_dp = boxed.shape[0]
    prods = [
        pltpu.VMEM((turns,) + (2,) * bits + (rows, width), jnp.bfloat16) for width in widths
    ]
    recvs = [
        pltpu.VMEM((turns,) + (2,) * (bits - 1 - step) + (rows, width), jnp.bfloat16)
        for width in widths
        for step in range(bits)
    ]
    vmem = pl.BlockSpec(memory_space=pltpu.VMEM)
    kernel = lambda *refs: grad_kernel(axis_bits, orders, widths, subs, n_dp, *refs)
    return pl.pallas_call(
        kernel,
        out_shape=(
            jax.ShapeDtypeStruct((rows, hidden), jnp.float32),
            jax.ShapeDtypeStruct((rows, hidden), jnp.float32),
            jax.ShapeDtypeStruct(boxed.shape, boxed.dtype),
        ),
        in_specs=[vmem] * 5,
        out_specs=(vmem, vmem, vmem),
        scratch_shapes=prods
        + recvs
        + [
            pltpu.SemaphoreType.DMA((len(orders), turns, bits)),
            pltpu.SemaphoreType.DMA((len(orders), turns, bits)),
            pltpu.SemaphoreType.DMA((n_dp,)),
            pltpu.SemaphoreType.DMA((n_dp,)),
        ],
        compiler_params=pltpu.CompilerParams(
            collective_id=0, has_side_effects=True, vmem_limit_bytes=24 * 1024 * 1024
        ),
        cost_estimate=pl.CostEstimate(
            flops=4 * xt.shape[0] * depth * hidden, bytes_accessed=1 << 24, transcendentals=0
        ),
        name="grad_sums",
    )(xt, ct, dh, act, boxed)


def part_orders(bits):
    group, near, next_near = bits - 1, bits - 2, bits - 3
    rest = [bit for bit in range(bits - 4, -1, -1)]
    return [
        [near, group, next_near] + rest,
        [group, near, next_near] + rest,
        [next_near, group, near] + rest,
    ]


def local(
    ref_image,
    ref_text,
    learner_image,
    learner_text,
    patches,
    cotangent,
    w_up,
    w_down,
    counts,
    sel_index,
    sel_dest,
):
    tensor_at = lax.axis_index("tensor")
    dp_at = lax.axis_index("dp")
    n_dp = lax.axis_size("dp")
    slots = sel_index.shape[0]
    cap = max(2, 2 * slots // n_dp)
    patch_rows, half_width = (patches.shape[1], patches.shape[2])
    count = slots * patch_rows
    half_x = patches[sel_index].reshape(count, half_width)
    half_cot = cotangent[sel_index].reshape(count, half_width)

    scores, xt, ct, act, grad_pre = shard_learnability(
        ref_image, ref_text, learner_image, learner_text, half_x, half_cot, w_up, w_down, n_dp
    )

    def down(side):
        columns = lax.dynamic_slice_in_dim(w_down, side * half_width, half_width, 1)
        return jnp.dot(act, columns, preferred_element_type=jnp.float32)

    came = swap(down(1 - tensor_at).astype(jnp.bfloat16), ("tensor",), (1,))
    out = (half_x.astype(jnp.float32) + (down(tensor_at) + came.astype(jnp.float32))).astype(
        jnp.bfloat16
    )
    live = jnp.arange(slots, dtype=jnp.int32) < counts[0]
    target = sel_dest[:, 0]
    earlier = jnp.arange(slots)[:, None] > jnp.arange(slots)[None, :]
    rank = jnp.sum(
        (earlier & (target[:, None] == target[None, :]) & live[None, :]).astype(jnp.int32), axis=1
    )
    bucket = (target ^ dp_at) * cap + rank
    slot_row = jnp.repeat(jnp.where(live, bucket, -1), patch_rows) * patch_rows + jnp.tile(
        jnp.arange(patch_rows, dtype=jnp.int32), slots
    )
    placer = (
        jnp.arange(n_dp * cap * patch_rows, dtype=jnp.int32)[:, None] == slot_row[None, :]
    ).astype(jnp.bfloat16)
    boxed = jnp.dot(placer, out, preferred_element_type=jnp.float32).astype(jnp.bfloat16)
    boxed = boxed.reshape(n_dp, cap * patch_rows, half_width)

    pairs = learner_image.shape[0]
    learnability = scores[0, 0, :pairs]
    other_scores = scores[1, 0, :pairs]
    shard_scores = jnp.concatenate(
        [
            jnp.where(tensor_at == 0, learnability, other_scores),
            jnp.where(tensor_at == 0, other_scores, learnability),
        ]
    )
    picked = sel_index[:, None] == jnp.arange(patches.shape[0], dtype=jnp.int32)[None, :]
    score_sel = jnp.sum(jnp.where(picked, shard_scores[None, :], 0.0), axis=1)
    weight = jnp.where(live, jax.nn.sigmoid(score_sel), 0.0)
    row_weight = jnp.repeat(weight, patch_rows)[:, None]

    axis_bits = [("dp", 1 << bit) for bit in range(n_dp.bit_length() - 2, -1, -1)] + [("group", 1)]
    dh = (row_weight * grad_pre.astype(jnp.float32)).astype(jnp.bfloat16)
    weighted_act = (row_weight * act.astype(jnp.float32)).astype(jnp.bfloat16)
    grad_up, grad_down_t, landed = gradients(
        xt, ct, dh, weighted_act, boxed, axis_bits
    )
    routed = landed.reshape(n_dp * cap, patch_rows, half_width)
    return (learnability, routed, grad_up, grad_down_t)


def solution(mesh):
    placed = (
        P(("dp", "tensor"), None),
        P(("dp", "tensor"), None),
        P(("dp", "tensor"), None),
        P(("dp", "tensor"), None),
        P("dp", "group", "tensor"),
        P("dp", "group", "tensor"),
        P(None, "tensor"),
        P("tensor", None),
        P("dp"),
        P("dp"),
        P("dp", None),
    )
    return jax.shard_map(
        local,
        mesh=mesh,
        in_specs=placed,
        out_specs=(
            P(("dp", "tensor")),
            P("dp", "group", "tensor"),
            P(("dp", "group"), "tensor"),
            P(("dp", "group"), "tensor"),
        ),
        check_vma=False,
    )
```
